128 devices in a mesh: dp: 128 (over z, x, y, core).
Axes of the slice: x: 4, y: 4, z: 4, core: 2. Of those that a mesh axis runs over, the one named last changes fastest.
Arguments:
- frames: bfloat16 [262144, 1024], P('dp'), may hold values from -8 to 8
- min_dist: float32 [262144], P('dp'), may hold values from 256 to 7680, as said below
- cand_index: int32 [2, 128, 16], P(None, 'dp'), may hold values from 0 to 2047, as said below
- cand_count: int32 [2, 128], replicated, may hold values from 1 to 16, as said below
Outputs:
- new_dist: float32 [262144], P('dp')
- weights: float32 [2, 2048], P(None, 'dp')
- costs: float32 [2], replicated
The draws below stay inside these ranges and needn't reach their ends.
Inputs may be any that keep to these rules, and one draw needn't show every extreme that they name: `cand_index`: row numbers within one device's 2048 frames; entries of empty slots are row numbers too. `cand_count`: in every round some device fills all 16 slots and some other device fills one. `min_dist`: positive distances.
All inputs are finite; a program needn't handle non-finite values.
Results may differ from the reference program's by a relative error of at most 0.0003.
Values may be sent and summed in bfloat16 or wider, within the bound.
No kernel may reach another device: no remote copies, remote signals or barrier semaphores. Data moves between devices by JAX's collectives and lax.ppermute only.
A program may use at most 128 MiB of HBM per device.

```python
import jax
import jax.numpy as jnp
from jax import lax

D = 1024
FR_DEV = 2048
SLOTS = 16
ROUNDS = 2
FRAMES = 262144
CANDS = 2048
N_DP = 128


def draw_frames(key, part):
    key = jax.random.fold_in(key, 11)
    key_c = jax.random.fold_in(key, 2)
    values = jax.random.normal(key_c, (FRAMES, D), jnp.float32)
    return jnp.clip(values, -8.0, 8.0).astype(jnp.bfloat16)


def draw_min_dist(key, part):
    key = jax.random.fold_in(key, 23)
    owner = (jnp.arange(FRAMES) // FR_DEV).astype(jnp.float32)
    rise = 1.0 + 2.0 * owner / max(N_DP - 1, 1)
    base = jax.random.uniform(key, (FRAMES,), jnp.float32, 0.25, 2.5)
    return (base * rise * D).astype(jnp.float32)


def draw_cand_index(key, part):
    key = jax.random.fold_in(key, 37)
    picks = jax.random.randint(key, (ROUNDS, N_DP, SLOTS), 0, FR_DEV)
    picks = picks.at[0, 0, 0].set(FR_DEV - 1)
    picks = picks.at[0, 0, 1].set(0)
    return picks.astype(jnp.int32)


def draw_cand_count(key, part):
    key = jax.random.fold_in(key, 41)
    key_a, key_b = jax.random.split(key)
    counts = jax.random.randint(key_a, (ROUNDS, N_DP), 1, SLOTS + 1)
    full = jax.random.randint(key_b, (ROUNDS, 1), 0, N_DP)
    single = (full + 1) % N_DP
    position = jnp.arange(N_DP)[None, :]
    counts = jnp.where(position == full, SLOTS, counts)
    counts = jnp.where(position == single, 1, counts)
    return counts.astype(jnp.int32)


def setup_inputs(seed: int = 0) -> dict:
    key_of = jax.random.split(jax.random.key(seed), 5)
    return {
        "frames": draw_frames(jax.random.fold_in(key_of[4], 71), 0),
        "min_dist": draw_min_dist(jax.random.fold_in(key_of[4], 71), 0),
        "cand_index": draw_cand_index(jax.random.fold_in(key_of[4], 71), 0),
        "cand_count": draw_cand_count(jax.random.fold_in(key_of[4], 71), 0),
    }


def reference(frames, min_dist, cand_index, cand_count):
    sq_norm = jnp.sum(jnp.square(frames.astype(jnp.float32)), axis=1)
    offsets = (jnp.arange(N_DP) * FR_DEV).astype(jnp.int32)
    slot_ids = jnp.arange(CANDS) % SLOTS
    owner_ids = jnp.arange(CANDS) // SLOTS
    factor = 16.0 / D
    running = min_dist
    weight_list = []
    cost_list = []
    blocks_x = frames.reshape(N_DP, FR_DEV, D)
    blocks_n = sq_norm.reshape(N_DP, FR_DEV)
    for rnd in range(ROUNDS):
        rows = (cand_index[rnd] + offsets[:, None]).reshape(CANDS).astype(jnp.int32)
        cands = frames[rows]
        cand_norm = sq_norm[rows]
        live = slot_ids < cand_count[rnd][owner_ids]
        blocks_r = running.reshape(N_DP, FR_DEV)

        def one_block(items):
            block_x, block_n, block_r = items
            inner = jnp.dot(block_x, cands.T, preferred_element_type=jnp.float32)
            dist = jnp.maximum(block_n[:, None] + cand_norm[None, :] - 2.0 * inner, 0.0)
            dist = jnp.where(live[None, :], dist, jnp.inf)
            near = jnp.min(dist, axis=1)
            share = jnp.exp(-(dist - near[:, None]) * factor)
            share = share / jnp.sum(share, axis=1, keepdims=True)
            return jnp.minimum(block_r, near), jnp.sum(share, axis=0)

        updated, partial_w = lax.map(one_block, (blocks_x, blocks_n, blocks_r))
        running = updated.reshape(FRAMES)
        weight_list.append(jnp.sum(partial_w, axis=0) * (SLOTS / FR_DEV))
        cost_list.append(jnp.sum(running) / (FRAMES * D))
    return running, jnp.stack(weight_list), jnp.stack(cost_list)
```

```python
import functools
import math

import jax
import jax.numpy as jnp
import numpy as np
from jax import lax
from jax.experimental import pallas as pl
from jax.experimental.pallas import tpu as pltpu
from jax.sharding import PartitionSpec as P

DIMS = (4, 4, 4)
CORES = 2
ORDERS = ((2, 1, 0), (0, 2, 1))
OFFSETS = (0, -1, 1, 2)


def device_id(pos, core):
    return ((pos[0] * DIMS[1] + pos[1]) * DIMS[2] + pos[2]) * CORES + core


def all_positions():
    for z in range(DIMS[0]):
        for x in range(DIMS[1]):
            for y in range(DIMS[2]):
                yield (z, x, y)


def moved(pos, axis, by):
    out = list(pos)
    out[axis] = (out[axis] + by) % DIMS[axis]
    return tuple(out)


def stage_perm(stage, offset):
    pairs = []
    for pos in all_positions():
        for core in range(CORES):
            source = moved(pos, ORDERS[core][stage], offset)
            pairs.append((device_id(source, core), device_id(pos, core)))
    return pairs


def swap_perm():
    return [
        (device_id(pos, core), device_id(pos, 1 - core))
        for pos in all_positions()
        for core in range(CORES)
    ]


def owner_table():
    table = np.zeros((DIMS[0] * DIMS[1] * DIMS[2] * CORES,) * 2, np.int32)
    for pos in all_positions():
        for core in range(CORES):
            row = []
            for parity in (core, 1 - core):
                order = ORDERS[parity]
                for o3 in OFFSETS:
                    for o2 in OFFSETS:
                        for o1 in OFFSETS:
                            src = moved(pos, order[2], o3)
                            src = moved(src, order[1], o2)
                            src = moved(src, order[0], o1)
                            row.append(device_id(src, parity))
            table[device_id(pos, core)] = row
    return table


def ring_stage(block, stage):
    return [block] + [
        lax.ppermute(block, "dp", stage_perm(stage, off)) for off in OFFSETS[1:]
    ]


LANES = 256
PIECE = 256


def round_kernel(
    slots, factor, owner_ref, count_ref, *refs,
):
    pieces, refs = refs[:8], refs[8:]
    ft_ref, sq_ref, run_ref = refs[:3]
    out_w_ref, out_run_ref, out_cost_ref = refs[3:6]
    dist_refs, refs = refs[6:9], refs[9:]
    norm_ref, acc_ref, sorted_ref = refs
    cands = PIECE * 8
    blocks = ft_ref.shape[1] // LANES
    groups = PIECE // slots

    for j, piece in enumerate(pieces):
        def norm_step(g, carry, j=j, piece=piece):
            rows = piece[pl.ds(pl.multiple_of(g * slots, slots), slots), :].astype(jnp.float32)
            norm = jnp.sum(rows * rows, axis=1, keepdims=True)
            limit = count_ref[owner_ref[0, j * groups + g]]
            slot = lax.broadcasted_iota(jnp.int32, (slots, 128), 0)
            wide = jnp.where(slot < limit, jnp.broadcast_to(norm, (slots, 128)), jnp.inf)
            norm_ref[pl.ds(pl.multiple_of(j * PIECE + g * slots, slots), slots), :] = wide
            return carry
        lax.fori_loop(0, groups, norm_step, 0, unroll=4)

    acc_ref[...] = jnp.zeros_like(acc_ref)
    scale = factor * math.log2(math.e)
    near = {}
    recip = {}

    def fold_rows(x, op):
        parts = [x[k * 8:(k + 1) * 8, :] for k in range(x.shape[0] // 8)]
        while len(parts) > 1:
            parts = [op(a, b) for a, b in zip(parts[::2], parts[1::2])]
        return parts[0]

    for t in range(blocks + 2):
        a, b, c = t, t - 1, t - 2
        lowest = jnp.full((8, LANES), jnp.inf, jnp.float32)
        total = jnp.zeros((8, LANES), jnp.float32)
        if a < blocks:
            ft = ft_ref[:, a * LANES:(a + 1) * LANES]
            sq = sq_ref[:, a * LANES:(a + 1) * LANES]
        for j in range(8):
            rows = slice(j * PIECE, (j + 1) * PIECE)
            if a < blocks:
                inner = jnp.dot(pieces[j][...], ft, preferred_element_type=jnp.float32)
                norm = norm_ref[rows, :]
                norm = jnp.concatenate([norm, norm], axis=1)
                dist = jnp.maximum((norm + sq) + inner, 0.0)
                dist_refs[a % 3][rows, :] = dist
                lowest = jnp.minimum(lowest, fold_rows(dist, jnp.minimum))
            if 0 <= b < blocks:
                e = jnp.exp2((near[b] - dist_refs[b % 3][rows, :]) * scale)
                dist_refs[b % 3][rows, :] = e
                total = total + fold_rows(e, jnp.add)
            if 0 <= c:
                share = dist_refs[c % 3][rows, :] * recip[c]
                acc_ref[rows, :] += share[:, :128] + share[:, 128:]
        if a < blocks:
            near[a] = jnp.min(lowest, axis=0, keepdims=True)
            lanes = slice(a * LANES, (a + 1) * LANES)
            out_run_ref[:, lanes] = jnp.minimum(run_ref[:, lanes], near[a])
        if 0 <= b < blocks:
            recip[b] = 1.0 / jnp.sum(total, axis=0, keepdims=True)

    def place(g, carry):
        to = pl.multiple_of(owner_ref[0, g] * slots, slots)
        sorted_ref[pl.ds(to, slots), :] = acc_ref[pl.ds(pl.multiple_of(g * slots, slots), slots), :]
        return carry
    lax.fori_loop(0, cands // slots, place, 0, unroll=4)
    sums = lax.dot_general(
        jnp.ones((8, 128), jnp.float32), sorted_ref[...], (((1,), (1,)), ((), ())),
        precision=lax.Precision.HIGHEST, preferred_element_type=jnp.float32,
    )
    out_w_ref[...] = sums[:1, :] * (slots / ft_ref.shape[1])
    out_cost_ref[...] = jnp.sum(out_run_ref[...], axis=1, keepdims=True)


def run_round(pieces, ft, sq, running, owner, counts, slots, factor):
    frames = ft.shape[1]
    cands = PIECE * 8
    vmem = pl.BlockSpec(memory_space=pltpu.VMEM)
    smem = pl.BlockSpec(memory_space=pltpu.SMEM)
    return pl.pallas_call(
        functools.partial(round_kernel, slots, factor),
        out_shape=(
            jax.ShapeDtypeStruct((1, cands), jnp.float32),
            jax.ShapeDtypeStruct((1, frames), jnp.float32),
            jax.ShapeDtypeStruct((1, 1), jnp.float32),
        ),
        in_specs=[smem, smem] + [vmem] * 11,
        out_specs=(vmem, vmem, vmem),
        scratch_shapes=[pltpu.VMEM((cands, LANES), jnp.float32)] * 3
        + [pltpu.VMEM((cands, 128), jnp.float32)] * 3,
        compiler_params=pltpu.CompilerParams(vmem_limit_bytes=32 * 1024 * 1024),
        cost_estimate=pl.CostEstimate(
            flops=2 * cands * frames * ft.shape[0],
            bytes_accessed=8 * 1024 * 1024,
            transcendentals=cands * frames,
        ),
    )(owner, counts, *pieces, ft, sq, running)


def body(frames, min_dist, cand_index, cand_count):
    fr_dev, width = frames.shape
    rounds, _, slots = cand_index.shape
    devices = lax.axis_size("dp")
    me = lax.axis_index("dp")
    factor = 16.0 / width

    wanted = cand_index[:, 0, :].reshape(rounds * slots, 1)
    hot = (wanted == lax.broadcasted_iota(jnp.int32, (rounds * slots, fr_dev), 1)).astype(jnp.bfloat16)
    rows = jnp.dot(hot, frames, preferred_element_type=jnp.float32).astype(jnp.bfloat16)

    block = rows
    block = jnp.concatenate(ring_stage(block, 0), axis=0)
    block = jnp.concatenate(ring_stage(block, 1), axis=0)
    block = block.reshape(16, rounds, slots, width)
    parts = [block[:, r].reshape(16 * slots, width) for r in range(rounds)]

    sq = jnp.sum(jnp.square(frames.astype(jnp.float32)), axis=1).reshape(1, fr_dev)
    ft = (frames * jnp.bfloat16(-2.0)).T
    owner = lax.dynamic_slice_in_dim(jnp.asarray(owner_table()), me, 1, 0)

    running = min_dist.reshape(1, fr_dev)
    weights, costs = [], []
    after = None
    for r in range(rounds):
        part = parts[r]
        if after is not None:
            part = lax.optimization_barrier((part, after))[0]
        mine = ring_stage(part, 2)
        after = mine[-1]
        theirs = [lax.ppermute(p, "dp", swap_perm()) for p in mine]
        w, running, cost = run_round(
            mine + theirs, ft, sq, running, owner, cand_count[r], slots, factor
        )
        weights.append(w)
        costs.append(cost)
    scale = 1.0 / (fr_dev * devices * width)
    sheet = [w.reshape(devices, slots) for w in weights]
    sheet += [jnp.broadcast_to(c * scale, (devices, slots)) for c in costs]
    sheet = jnp.concatenate(sheet, axis=1)
    sheet = lax.all_to_all(sheet, "dp", 0, 0, tiled=True)
    sums = jnp.sum(sheet, axis=0)
    mine = sums[: rounds * slots].reshape(rounds, slots)
    costs = sums[rounds * slots:].reshape(rounds, slots)[:, 0]
    return (running.reshape(fr_dev), mine, costs)


def solution(mesh):
    return jax.shard_map(
        body,
        mesh=mesh,
        in_specs=(P("dp", None), P("dp"), P(None, "dp", None), P()),
        out_specs=(P("dp"), P(None, "dp"), P()),
        check_vma=False,
    )
```

```python
import functools
import math

import jax
import jax.numpy as jnp
import numpy as np
from jax import lax
from jax.experimental import pallas as pl
from jax.experimental.pallas import tpu as pltpu
from jax.sharding import PartitionSpec as P

DIMS = (4, 4, 4)
CORES = 2
ORDERS = ((2, 1, 0), (0, 2, 1))
OFFSETS = (0, -1, 1, 2)


def device_id(pos, core):
    return ((pos[0] * DIMS[1] + pos[1]) * DIMS[2] + pos[2]) * CORES + core


def all_positions():
    for z in range(DIMS[0]):
        for x in range(DIMS[1]):
            for y in range(DIMS[2]):
                yield (z, x, y)


def moved(pos, axis, by):
    out = list(pos)
    out[axis] = (out[axis] + by) % DIMS[axis]
    return tuple(out)


def stage_perm(stage, offset):
    pairs = []
    for pos in all_positions():
        for core in range(CORES):
            source = moved(pos, ORDERS[core][stage], offset)
            pairs.append((device_id(source, core), device_id(pos, core)))
    return pairs


def swap_perm():
    return [
        (device_id(pos, core), device_id(pos, 1 - core))
        for pos in all_positions()
        for core in range(CORES)
    ]


def owner_table():
    table = np.zeros((DIMS[0] * DIMS[1] * DIMS[2] * CORES,) * 2, np.int32)
    for pos in all_positions():
        for core in range(CORES):
            row = []
            for parity in (core, 1 - core):
                order = ORDERS[parity]
                for o3 in OFFSETS:
                    for o2 in OFFSETS:
                        for o1 in OFFSETS:
                            src = moved(pos, order[2], o3)
                            src = moved(src, order[1], o2)
                            src = moved(src, order[0], o1)
                            row.append(device_id(src, parity))
            table[device_id(pos, core)] = row
    return table


def ring_stage(block, stage):
    return [block] + [
        lax.ppermute(block, "dp", stage_perm(stage, off)) for off in OFFSETS[1:]
    ]


LANES = 256
SIZES = (1152, 1280)


def fold_rows(x, op):
    parts = [x[k * 8:(k + 1) * 8, :] for k in range(x.shape[0] // 8)]
    while len(parts) > 1:
        paired = [op(a, b) for a, b in zip(parts[::2], parts[1::2])]
        parts = paired + parts[len(parts) - len(parts) % 2:]
    return parts[0]


def round_kernel(slots, factor, n_pieces, owner_ref, count_ref, *refs):
    pieces, refs = refs[:n_pieces], refs[n_pieces:]
    frames_ref, sq_ref, run_ref, out_w_ref, out_run_ref, out_cost_ref = refs[:6]
    wide_ref, cand_ref, frame_ref, even_ref, odd_ref, norm_ref, acc_ref, sorted_ref, sem = refs[6:]
    cands, width = cand_ref.shape
    rows_each = cands // n_pieces
    blocks = frame_ref.shape[0] // LANES
    groups = rows_each // slots

    copy = pltpu.make_async_copy(frames_ref, frame_ref, sem)
    copy.start()

    norm_ref[...] = jnp.full_like(norm_ref, jnp.inf)
    slot = lax.broadcasted_iota(jnp.int32, (slots, 128), 0)
    live = jnp.int32(0)
    for j, piece in enumerate(pieces):
        def close_up(g, at, j=j, piece=piece):
            rows = piece[pl.ds(pl.multiple_of(g * slots, slots), slots), :].astype(jnp.float32)
            norm = jnp.sum(rows * rows, axis=1, keepdims=True)
            limit = count_ref[owner_ref[0, j * groups + g]]
            norm = jnp.where(slot < limit, jnp.broadcast_to(norm, (slots, 128)), jnp.inf)
            norm_ref[pl.ds(at, slots), :] = norm
            for k in range(width // 128):
                wide_ref[k, pl.ds(at, slots), :] = rows[:, k * 128:(k + 1) * 128]
            return at + limit

        live = lax.fori_loop(0, groups, close_up, live, unroll=16)
    copy.wait()

    scale = factor * math.log2(math.e)

    def lanes(t):
        return pl.ds(pl.multiple_of(t * LANES, LANES), LANES)

    def all_blocks(size):
        chunk = size // 2
        part_rows = 128

        def narrow(i, carry):
            at = pl.multiple_of(i * part_rows, part_rows)
            kept = lax.broadcasted_iota(jnp.int32, (part_rows, 128), 0) + at < live
            for k in range(width // 128):
                x = jnp.where(kept, wide_ref[k, pl.ds(at, part_rows), :], 0.0)
                cand_ref[pl.ds(at, part_rows), k * 128:(k + 1) * 128] = x.astype(jnp.bfloat16)
            acc_ref[pl.ds(at, part_rows), :] = jnp.zeros((part_rows, 128), jnp.float32)
            return carry

        lax.fori_loop(0, size // part_rows, narrow, 0)

        def step(t, near, into, of):
            if into is not None:
                part = frame_ref[lanes(t + 1), :] * jnp.bfloat16(-2.0)
                sq = sq_ref[:, lanes(t + 1)]
                lowest = jnp.full((8, LANES), jnp.inf, jnp.float32)
            total = jnp.zeros((8, LANES), jnp.float32)
            for first in range(0, size, chunk):
                if into is not None:
                    rows = slice(first, first + chunk)
                    inner = lax.dot_general(
                        cand_ref[rows, :], part, (((1,), (1,)), ((), ())),
                        preferred_element_type=jnp.float32,
                    )
                    norm = norm_ref[rows, :]
                    norm = jnp.concatenate([norm, norm], axis=1)
                    dist = jnp.maximum((norm + sq) + inner, 0.0)
                    into[rows, :] = dist
                    lowest = jnp.minimum(lowest, fold_rows(dist, jnp.minimum))
                if of is not None:
                    for r in range(first, first + chunk, chunk // 4):
                        e = jnp.exp2((near - of[r:r + chunk // 4, :]) * scale)
                        of[r:r + chunk // 4, :] = e
                        total = total + fold_rows(e, jnp.add)
            if of is not None:
                recip = 1.0 / jnp.sum(total, axis=0, keepdims=True)
                for r in range(0, size, chunk // 4):
                    share = of[r:r + chunk // 4, :] * recip
                    acc_ref[r:r + chunk // 4, :] += share[:, :128] + share[:, 128:]
            if into is None:
                return None
            near = jnp.min(lowest, axis=0, keepdims=True)
            out_run_ref[:, lanes(t + 1)] = jnp.minimum(run_ref[:, lanes(t + 1)], near)
            return near

        def pair(i, near):
            near = step(2 * i, near, odd_ref, even_ref)
            return step(2 * i + 1, near, even_ref, odd_ref)

        near = step(-1, None, even_ref, None)
        near = lax.fori_loop(0, blocks // 2 - 1, pair, near)
        near = step(blocks - 2, near, odd_ref, even_ref)
        step(blocks - 1, near, None, odd_ref)

    above = jnp.int32(0)
    for size in [s for s in SIZES if s < cands] + [cands]:
        pl.when(jnp.logical_and(live > above, live <= size))(functools.partial(all_blocks, size))
        above = size

    def place(g, at):
        to = pl.multiple_of(owner_ref[0, g] * slots, slots)
        limit = count_ref[owner_ref[0, g]]
        mine = acc_ref[pl.ds(at, slots), :]
        sorted_ref[pl.ds(to, slots), :] = jnp.where(slot < limit, mine, 0.0)
        return at + limit

    lax.fori_loop(0, cands // slots, place, jnp.int32(0), unroll=4)
    sums = lax.dot_general(
        jnp.ones((8, 128), jnp.float32), sorted_ref[...], (((1,), (1,)), ((), ())),
        precision=lax.Precision.HIGHEST, preferred_element_type=jnp.float32,
    )
    out_w_ref[...] = sums[:1, :] * (slots / frame_ref.shape[0])
    out_cost_ref[...] = jnp.sum(out_run_ref[...], axis=1, keepdims=True)


def run_round(pieces, frames, sq, running, owner, counts, slots, factor):
    fr_dev, width = frames.shape
    cands = sum(p.shape[0] for p in pieces)
    vmem = pl.BlockSpec(memory_space=pltpu.VMEM)
    smem = pl.BlockSpec(memory_space=pltpu.SMEM)
    hbm = pl.BlockSpec(memory_space=pl.ANY)
    return pl.pallas_call(
        functools.partial(round_kernel, slots, factor, len(pieces)),
        out_shape=(
            jax.ShapeDtypeStruct((1, cands), jnp.float32),
            jax.ShapeDtypeStruct((1, fr_dev), jnp.float32),
            jax.ShapeDtypeStruct((1, 1), jnp.float32),
        ),
        in_specs=[smem, smem] + [vmem] * len(pieces) + [hbm] + [vmem] * 2,
        out_specs=(vmem, vmem, vmem),
        scratch_shapes=[
            pltpu.VMEM((width // 128, cands + slots, 128), jnp.float32),
            pltpu.VMEM((cands, width), jnp.bfloat16),
            pltpu.VMEM((fr_dev, width), jnp.bfloat16),
            pltpu.VMEM((cands, LANES), jnp.float32),
            pltpu.VMEM((cands, LANES), jnp.float32),
            pltpu.VMEM((cands + slots, 128), jnp.float32),
            pltpu.VMEM((cands + slots, 128), jnp.float32),
            pltpu.VMEM((cands, 128), jnp.float32),
            pltpu.SemaphoreType.DMA,
        ],
        compiler_params=pltpu.CompilerParams(vmem_limit_bytes=50 * 1024 * 1024),
        cost_estimate=pl.CostEstimate(
            flops=2 * cands * fr_dev * width,
            bytes_accessed=8 * 1024 * 1024,
            transcendentals=cands * fr_dev,
        ),
    )(owner, counts, *pieces, frames, sq, running)


def body(frames, min_dist, cand_index, cand_count):
    fr_dev, width = frames.shape
    rounds, _, slots = cand_index.shape
    devices = lax.axis_size("dp")
    me = lax.axis_index("dp")
    factor = 16.0 / width

    wanted = cand_index[:, 0, :].reshape(rounds * slots, 1)
    hot = (wanted == lax.broadcasted_iota(jnp.int32, (rounds * slots, fr_dev), 1)).astype(jnp.bfloat16)
    rows = jnp.dot(hot, frames, preferred_element_type=jnp.float32).astype(jnp.bfloat16)

    sq = jnp.sum(jnp.square(frames.astype(jnp.float32)), axis=1).reshape(1, fr_dev)
    owner = lax.dynamic_slice_in_dim(jnp.asarray(owner_table()), me, 1, 0)

    block = jnp.concatenate(ring_stage(rows, 0), axis=0)
    block, sq, owner = lax.optimization_barrier((block, sq, owner))
    block = jnp.concatenate(ring_stage(block, 1), axis=0)
    block = block.reshape(16, rounds, slots, width)
    parts = [block[:, r].reshape(16 * slots, width) for r in range(rounds)]

    running = min_dist.reshape(1, fr_dev)
    weights, costs = [], []
    gathered, swapped = [], []
    for r in range(rounds):
        part = parts[r]
        if r > 0:
            part, _ = lax.optimization_barrier((part, (gathered[-1], swapped[-1][:3])))
        mine = ring_stage(part, 2)
        if r > 0:
            mine, weights[-1] = lax.optimization_barrier((mine, weights[-1]))
        theirs = [lax.ppermute(p, "dp", swap_perm()) for p in mine]
        gathered.append(mine)
        swapped.append(theirs)
        w, running, cost = run_round(
            mine + theirs, frames, sq, running, owner, cand_count[r], slots, factor
        )
        weights.append(w)
        costs.append(cost)
    scale = 1.0 / (fr_dev * devices * width)
    sheet = [w.reshape(devices, slots) for w in weights]
    sheet += [jnp.broadcast_to(c * scale, (devices, slots)) for c in costs]
    sheet = jnp.concatenate(sheet, axis=1)
    sheet = lax.all_to_all(sheet, "dp", 0, 0, tiled=True)
    sums = jnp.sum(sheet, axis=0)
    mine = sums[: rounds * slots].reshape(rounds, slots)
    costs = sums[rounds * slots:].reshape(rounds, slots)[:, 0]
    return (running.reshape(fr_dev), mine, costs)


def solution(mesh):
    return jax.shard_map(
        body,
        mesh=mesh,
        in_specs=(P("dp", None), P("dp"), P(None, "dp", None), P()),
        out_specs=(P("dp"), P(None, "dp"), P()),
        check_vma=False,
    )
```

```python
import functools
import math

import jax
import jax.numpy as jnp
import numpy as np
from jax import lax
from jax.experimental import pallas as pl
from jax.experimental.pallas import tpu as pltpu
from jax.sharding import PartitionSpec as P

DIMS = (4, 4, 4)
CORES = 2
ORDERS = ((2, 1, 0), (0, 2, 1))
OFFSETS = (0, -1, 1, 2)


def device_id(pos, core):
    return ((pos[0] * DIMS[1] + pos[1]) * DIMS[2] + pos[2]) * CORES + core


def all_positions():
    for z in range(DIMS[0]):
        for x in range(DIMS[1]):
            for y in range(DIMS[2]):
                yield (z, x, y)


def moved(pos, axis, by):
    out = list(pos)
    out[axis] = (out[axis] + by) % DIMS[axis]
    return tuple(out)


def stage_perm(stage, offset):
    pairs = []
    for pos in all_positions():
        for core in range(CORES):
            source = moved(pos, ORDERS[core][stage], offset)
            pairs.append((device_id(source, core), device_id(pos, core)))
    return pairs


def swap_perm():
    return [
        (device_id(pos, core), device_id(pos, 1 - core))
        for pos in all_positions()
        for core in range(CORES)
    ]


def owner_table():
    table = np.zeros((DIMS[0] * DIMS[1] * DIMS[2] * CORES,) * 2, np.int32)
    for pos in all_positions():
        for core in range(CORES):
            row = []
            for parity in (core, 1 - core):
                order = ORDERS[parity]
                for o3 in OFFSETS:
                    for o2 in OFFSETS:
                        for o1 in OFFSETS:
                            src = moved(pos, order[2], o3)
                            src = moved(src, order[1], o2)
                            src = moved(src, order[0], o1)
                            row.append(device_id(src, parity))
            table[device_id(pos, core)] = row
    return table


def ring_stage(block, stage):
    return [block] + [
        lax.ppermute(block, "dp", stage_perm(stage, off)) for off in OFFSETS[1:]
    ]


LANES = 256
COST_LANE = 120
SIZES = (1152, 1280)


def fold_rows(x, op):
    parts = [x[k * 8:(k + 1) * 8, :] for k in range(x.shape[0] // 8)]
    while len(parts) > 1:
        paired = [op(a, b) for a, b in zip(parts[::2], parts[1::2])]
        parts = paired + parts[len(parts) - len(parts) % 2:]
    return parts[0]


def round_kernel(slots, factor, rnd, weight_scale, cost_scale, n_pieces, owner_ref, count_ref, *refs):
    pieces, refs = refs[:n_pieces], refs[n_pieces:]
    frame_ref, sq_ref, run_ref, sheet_ref, out_run_ref, out_sheet_ref = refs[:6]
    wide_ref, cand_ref, even_ref, odd_ref, norm_ref, acc_ref, sorted_ref = refs[6:]
    cands, width = cand_ref.shape
    rows_each = cands // n_pieces
    blocks = frame_ref.shape[0] // LANES
    groups = rows_each // slots

    live = jnp.int32(0)
    for j, piece in enumerate(pieces):
        def close_up(g, at, j=j, piece=piece):
            rows = piece[pl.ds(pl.multiple_of(g * slots, slots), slots), :].astype(jnp.float32)
            for k in range(width // 128):
                wide_ref[k, pl.ds(at, slots), :] = rows[:, k * 128:(k + 1) * 128]
            return at + count_ref[rnd, owner_ref[0, j * groups + g]]

        live = lax.fori_loop(0, groups, close_up, live, unroll=16)
    scale = factor * math.log2(math.e)

    def lanes(t):
        return pl.ds(pl.multiple_of(t * LANES, LANES), LANES)

    def all_blocks(size):
        chunk = size // 2
        part_rows = 128

        def narrow(i, carry):
            at = pl.multiple_of(i * part_rows, part_rows)
            kept = lax.broadcasted_iota(jnp.int32, (part_rows, 128), 0) + at < live
            squares = jnp.zeros((part_rows, 128), jnp.float32)
            for k in range(width // 128):
                x = jnp.where(kept, wide_ref[k, pl.ds(at, part_rows), :], 0.0)
                cand_ref[pl.ds(at, part_rows), k * 128:(k + 1) * 128] = x.astype(jnp.bfloat16)
                squares = squares + x * x
            norm = jnp.broadcast_to(jnp.sum(squares, axis=1, keepdims=True), (part_rows, 128))
            norm_ref[pl.ds(at, part_rows), :] = jnp.where(kept, norm, jnp.inf)
            acc_ref[pl.ds(at, part_rows), :] = jnp.zeros((part_rows, 128), jnp.float32)
            return carry

        parts = size // part_rows
        lax.fori_loop(0, parts, narrow, 0, unroll=3 if parts % 3 == 0 else 2)

        def step(t, near, into, of):
            if into is not None:
                part = frame_ref[lanes(t + 1), :]
                sq = sq_ref[:, lanes(t + 1)]
                lowest = jnp.full((8, LANES), jnp.inf, jnp.float32)
            total = jnp.zeros((8, LANES), jnp.float32)
            for first in range(0, size, chunk):
                if into is not None:
                    rows = slice(first, first + chunk)
                    inner = lax.dot_general(
                        cand_ref[rows, :], part, (((1,), (1,)), ((), ())),
                        preferred_element_type=jnp.float32,
                    )
                    norm = norm_ref[rows, :]
                    norm = jnp.concatenate([norm, norm], axis=1)
                    dist = jnp.maximum((norm + sq) + inner, 0.0)
                    into[rows, :] = dist
                    lowest = jnp.minimum(lowest, fold_rows(dist, jnp.minimum))
                if of is not None:
                    for r in range(first, first + chunk, chunk // 4):
                        e = jnp.exp2((near - of[r:r + chunk // 4, :]) * scale)
                        of[r:r + chunk // 4, :] = e
                        total = total + fold_rows(e, jnp.add)
            if of is not None:
                recip = 1.0 / jnp.sum(total, axis=0, keepdims=True)
                for r in range(0, size, chunk // 4):
                    share = of[r:r + chunk // 4, :] * recip
                    acc_ref[r:r + chunk // 4, :] += share[:, :128] + share[:, 128:]
            if into is None:
                return None
            near = jnp.min(lowest, axis=0, keepdims=True)
            out_run_ref[:, lanes(t + 1)] = jnp.minimum(run_ref[:, lanes(t + 1)], near)
            return near

        def pair(i, near):
            near = step(2 * i, near, odd_ref, even_ref)
            return step(2 * i + 1, near, even_ref, odd_ref)

        near = step(-1, None, even_ref, None)
        near = lax.fori_loop(0, blocks // 2 - 1, pair, near)
        near = step(blocks - 2, near, odd_ref, even_ref)
        step(blocks - 1, near, None, odd_ref)

    above = jnp.int32(0)
    for size in [s for s in SIZES if s < cands] + [cands]:
        pl.when(jnp.logical_and(live > above, live <= size))(functools.partial(all_blocks, size))
        above = size

    slot = lax.broadcasted_iota(jnp.int32, (slots, 128), 0)

    def place(g, at):
        to = pl.multiple_of(owner_ref[0, g] * slots, slots)
        limit = count_ref[rnd, owner_ref[0, g]]
        mine = acc_ref[pl.ds(at, slots), :]
        sorted_ref[pl.ds(to, slots), :] = jnp.where(slot < limit, mine, 0.0)
        return at + limit

    lax.fori_loop(0, cands // slots, place, jnp.int32(0), unroll=4)
    lane = lax.broadcasted_iota(jnp.int32, sheet_ref.shape, 1)
    sheet = sheet_ref[...] if rnd > 0 else jnp.zeros(sheet_ref.shape, jnp.float32)
    for s in range(slots):
        mine = sorted_ref[pl.ds(s, cands // slots, stride=slots), :]
        total = jnp.sum(mine, axis=1, keepdims=True) * weight_scale
        sheet = jnp.where(lane == rnd * slots + s, total, sheet)
    cost = jnp.sum(out_run_ref[...], axis=1, keepdims=True) * cost_scale
    out_sheet_ref[...] = jnp.where(lane == COST_LANE + rnd, cost, sheet)


def run_round(pieces, frames, sq, running, sheet, owner, counts, rnd, slots, factor, devices):
    fr_dev, width = frames.shape
    cands = sum(p.shape[0] for p in pieces)
    vmem = pl.BlockSpec(memory_space=pltpu.VMEM)
    smem = pl.BlockSpec(memory_space=pltpu.SMEM)
    kernel = functools.partial(
        round_kernel, slots, factor, rnd, slots / fr_dev, 1.0 / (fr_dev * devices * width), len(pieces)
    )
    return pl.pallas_call(
        kernel,
        out_shape=(
            jax.ShapeDtypeStruct((1, fr_dev), jnp.float32),
            jax.ShapeDtypeStruct(sheet.shape, jnp.float32),
        ),
        in_specs=[smem, smem] + [vmem] * (len(pieces) + 4),
        out_specs=(vmem, vmem),
        scratch_shapes=[
            pltpu.VMEM((width // 128, cands + slots, 128), jnp.float32),
            pltpu.VMEM((cands, width), jnp.bfloat16),
            pltpu.VMEM((cands, LANES), jnp.float32),
            pltpu.VMEM((cands, LANES), jnp.float32),
            pltpu.VMEM((cands, 128), jnp.float32),
            pltpu.VMEM((cands + slots, 128), jnp.float32),
            pltpu.VMEM((cands, 128), jnp.float32),
        ],
        compiler_params=pltpu.CompilerParams(vmem_limit_bytes=28 * 1024 * 1024),
        cost_estimate=pl.CostEstimate(
            flops=2 * cands * fr_dev * width,
            bytes_accessed=8 * 1024 * 1024,
            transcendentals=cands * fr_dev,
        ),
    )(owner, counts, *pieces, frames, sq, running, sheet)


def pick_kernel(index_ref, frames_ref, out_ref, near_ref, row_ref, sems):
    rounds, _, slots = index_ref.shape
    wanted = [index_ref[r, 0, s] for r in range(rounds) for s in range(slots)]
    copies = []
    for i, at in enumerate(wanted):
        rows = pl.ds(pl.multiple_of((at // 16) * 16, 16), 16)
        copies.append(pltpu.make_async_copy(frames_ref.at[rows], near_ref.at[i], sems.at[i]))
        copies[-1].start()
    row = lax.broadcasted_iota(jnp.int32, (16, frames_ref.shape[1]), 0)
    for i, at in enumerate(wanted):
        copies[i].wait()
        near = near_ref[i].astype(jnp.float32)
        row_ref[i:i + 1, :] = jnp.sum(jnp.where(row == at % 16, near, 0.0), axis=0, keepdims=True)
    out_ref[...] = row_ref[...].astype(jnp.bfloat16)


def pick_rows(frames, cand_index):
    count, width = cand_index.shape[0] * cand_index.shape[2], frames.shape[1]
    return pl.pallas_call(
        pick_kernel,
        out_shape=jax.ShapeDtypeStruct((count, width), frames.dtype),
        in_specs=[pl.BlockSpec(memory_space=pltpu.SMEM), pl.BlockSpec(memory_space=pl.ANY)],
        out_specs=pl.BlockSpec(memory_space=pltpu.VMEM),
        scratch_shapes=[
            pltpu.VMEM((count, 16, width), frames.dtype),
            pltpu.VMEM((count, width), jnp.float32),
            pltpu.SemaphoreType.DMA((count,)),
        ],
        compiler_params=pltpu.CompilerParams(vmem_limit_bytes=60 * 1024 * 1024),
        cost_estimate=pl.CostEstimate(flops=0, bytes_accessed=1024 * 1024, transcendentals=0),
    )(cand_index, frames)


def body(frames, min_dist, cand_index, cand_count):
    fr_dev, width = frames.shape
    rounds, _, slots = cand_index.shape
    devices = lax.axis_size("dp")
    me = lax.axis_index("dp")
    factor = 16.0 / width

    rows = pick_rows(frames, cand_index)
    block = jnp.concatenate(ring_stage(rows, 0), axis=0)
    block, frames = lax.optimization_barrier((block, frames))
    block = jnp.concatenate(ring_stage(block, 1), axis=0)

    sq = jnp.sum(jnp.square(frames.astype(jnp.float32)), axis=1).reshape(1, fr_dev)
    scaled = frames * jnp.bfloat16(-2.0)
    owner = lax.dynamic_slice_in_dim(jnp.asarray(owner_table()), me, 1, 0)
    block, sq, scaled, owner = lax.optimization_barrier((block, sq, scaled, owner))

    block = block.reshape(16, rounds, slots, width)
    parts = [block[:, r].reshape(16 * slots, width) for r in range(rounds)]

    running = min_dist.reshape(1, fr_dev)
    sheet = jnp.zeros((devices, 128), jnp.float32)
    gathered = []
    for r in range(rounds):
        part = parts[r]
        if r > 0:
            part, _ = lax.optimization_barrier((part, gathered[-1][1]))
        mine = ring_stage(part, 2)
        if r > 0:
            mine, sheet = lax.optimization_barrier((mine, sheet))
        theirs = [lax.ppermute(p, "dp", swap_perm()) for p in mine]
        gathered.append(mine)
        running, sheet = run_round(
            mine + theirs, scaled, sq, running, sheet, owner, cand_count, r, slots, factor, devices
        )
    sums = jnp.sum(lax.all_to_all(sheet, "dp", 0, 0, tiled=True), axis=0)
    mine = sums[: rounds * slots].reshape(rounds, slots)
    return (running.reshape(fr_dev), mine, sums[COST_LANE:COST_LANE + rounds])


def solution(mesh):
    return jax.shard_map(
        body,
        mesh=mesh,
        in_specs=(P("dp", None), P("dp"), P(None, "dp", None), P()),
        out_specs=(P("dp"), P(None, "dp"), P()),
        check_vma=False,
    )
```

```python
import functools
import math

import jax
import jax.numpy as jnp
import numpy as np
from jax import lax
from jax.experimental import pallas as pl
from jax.experimental.pallas import tpu as pltpu
from jax.sharding import PartitionSpec as P

DIMS = (4, 4, 4)
CORES = 2
LAST = (0, 1)
OFFSETS = (0, 2, -1, 1)


def device_id(pos, core):
    return ((pos[0] * DIMS[1] + pos[1]) * DIMS[2] + pos[2]) * CORES + core


def all_positions():
    for z in range(DIMS[0]):
        for x in range(DIMS[1]):
            for y in range(DIMS[2]):
                yield (z, x, y)


def moved(pos, axis, by):
    out = list(pos)
    out[axis] = (out[axis] + by) % DIMS[axis]
    return tuple(out)


def plane(pos, axis):
    return [p for p in all_positions() if p[axis] == pos[axis]]


def plane_groups():
    groups = []
    for core in range(CORES):
        for at in range(DIMS[LAST[core]]):
            pos = moved((0, 0, 0), LAST[core], at)
            groups.append([device_id(p, core) for p in plane(pos, LAST[core])])
    return groups


def last_perm(offset):
    pairs = []
    for pos in all_positions():
        for core in range(CORES):
            source = moved(pos, LAST[core], offset)
            pairs.append((device_id(source, core), device_id(pos, core)))
    return pairs


def swap_perm():
    return [
        (device_id(pos, core), device_id(pos, 1 - core))
        for pos in all_positions()
        for core in range(CORES)
    ]


def owner_table():
    table = np.zeros((DIMS[0] * DIMS[1] * DIMS[2] * CORES,) * 2, np.int32)
    for pos in all_positions():
        for core in range(CORES):
            row = []
            for parity in (core, 1 - core):
                for offset in OFFSETS:
                    there = moved(pos, LAST[parity], offset)
                    row += [device_id(p, parity) for p in plane(there, LAST[parity])]
            table[device_id(pos, core)] = row
    return table


def last_stage(block):
    return [block] + [lax.ppermute(block, "dp", last_perm(off)) for off in OFFSETS[1:]]


LANES = 256
COST_LANE = 120
SIZES = (1152, 1280)


def fold_rows(x, op):
    parts = [x[k * 8:(k + 1) * 8, :] for k in range(x.shape[0] // 8)]
    while len(parts) > 1:
        paired = [op(a, b) for a, b in zip(parts[::2], parts[1::2])]
        parts = paired + parts[len(parts) - len(parts) % 2:]
    return parts[0]


def round_kernel(slots, factor, rnd, weight_scale, cost_scale, n_pieces, owner_ref, count_ref, *refs):
    pieces, refs = refs[:n_pieces], refs[n_pieces:]
    frame_ref, sq_ref, run_ref, sheet_ref, out_run_ref, out_sheet_ref = refs[:6]
    wide_ref, cand_ref, even_ref, odd_ref, norm_ref, acc_ref, sorted_ref = refs[6:]
    cands, width = cand_ref.shape
    rows_each = cands // n_pieces
    blocks = frame_ref.shape[0] // LANES
    groups = rows_each // slots

    live = jnp.int32(0)
    for j, piece in enumerate(pieces):
        def close_up(g, at, j=j, piece=piece):
            rows = piece[pl.ds(pl.multiple_of(g * slots, slots), slots), :].astype(jnp.float32)
            for k in range(width // 128):
                wide_ref[k, pl.ds(at, slots), :] = rows[:, k * 128:(k + 1) * 128]
            return at + count_ref[rnd, owner_ref[0, j * groups + g]]

        live = lax.fori_loop(0, groups, close_up, live, unroll=16)
    scale = factor * math.log2(math.e)

    def lanes(t):
        return pl.ds(pl.multiple_of(t * LANES, LANES), LANES)

    def all_blocks(size):
        chunk = size // 2
        part_rows = 128

        def narrow(i, carry):
            at = pl.multiple_of(i * part_rows, part_rows)
            kept = lax.broadcasted_iota(jnp.int32, (part_rows, 128), 0) + at < live
            squares = jnp.zeros((part_rows, 128), jnp.float32)
            for k in range(width // 128):
                x = jnp.where(kept, wide_ref[k, pl.ds(at, part_rows), :], 0.0)
                cand_ref[pl.ds(at, part_rows), k * 128:(k + 1) * 128] = x.astype(jnp.bfloat16)
                squares = squares + x * x
            norm = jnp.broadcast_to(jnp.sum(squares, axis=1, keepdims=True), (part_rows, 128))
            norm_ref[pl.ds(at, part_rows), :] = jnp.where(kept, norm, jnp.inf)
            acc_ref[pl.ds(at, part_rows), :] = jnp.zeros((part_rows, 128), jnp.float32)
            return carry

        parts = size // part_rows
        lax.fori_loop(0, parts, narrow, 0, unroll=3 if parts % 3 == 0 else 2)

        def step(t, near, into, of):
            if into is not None:
                part = frame_ref[lanes(t + 1), :]
                sq = sq_ref[:, lanes(t + 1)]
                lowest = jnp.full((8, LANES), jnp.inf, jnp.float32)
            total = jnp.zeros((8, LANES), jnp.float32)
            for first in range(0, size, chunk):
                if into is not None:
                    rows = slice(first, first + chunk)
                    inner = lax.dot_general(
                        cand_ref[rows, :], part, (((1,), (1,)), ((), ())),
                        preferred_element_type=jnp.float32,
                    )
                    norm = norm_ref[rows, :]
                    norm = jnp.concatenate([norm, norm], axis=1)
                    dist = jnp.maximum((norm + sq) + inner, 0.0)
                    into[rows, :] = dist
                    lowest = jnp.minimum(lowest, fold_rows(dist, jnp.minimum))
                if of is not None:
                    for r in range(first, first + chunk, chunk // 4):
                        e = jnp.exp2((near - of[r:r + chunk // 4, :]) * scale)
                        of[r:r + chunk // 4, :] = e
                        total = total + fold_rows(e, jnp.add)
            if of is not None:
                recip = 1.0 / jnp.sum(total, axis=0, keepdims=True)
                for r in range(0, size, chunk // 4):
                    share = of[r:r + chunk // 4, :] * recip
                    acc_ref[r:r + chunk // 4, :] += share[:, :128] + share[:, 128:]
            if into is None:
                return None
            near = jnp.min(lowest, axis=0, keepdims=True)
            out_run_ref[:, lanes(t + 1)] = jnp.minimum(run_ref[:, lanes(t + 1)], near)
            return near

        def pair(i, near):
            near = step(2 * i, near, odd_ref, even_ref)
            return step(2 * i + 1, near, even_ref, odd_ref)

        near = step(-1, None, even_ref, None)
        near = lax.fori_loop(0, blocks // 2 - 1, pair, near)
        near = step(blocks - 2, near, odd_ref, even_ref)
        step(blocks - 1, near, None, odd_ref)

    above = jnp.int32(0)
    for size in [s for s in SIZES if s < cands] + [cands]:
        pl.when(jnp.logical_and(live > above, live <= size))(functools.partial(all_blocks, size))
        above = size

    slot = lax.broadcasted_iota(jnp.int32, (slots, 128), 0)

    def place(g, at):
        to = pl.multiple_of(owner_ref[0, g] * slots, slots)
        limit = count_ref[rnd, owner_ref[0, g]]
        mine = acc_ref[pl.ds(at, slots), :]
        sorted_ref[pl.ds(to, slots), :] = jnp.where(slot < limit, mine, 0.0)
        return at + limit

    lax.fori_loop(0, cands // slots, place, jnp.int32(0), unroll=4)
    lane = lax.broadcasted_iota(jnp.int32, sheet_ref.shape, 1)
    sheet = sheet_ref[...] if rnd > 0 else jnp.zeros(sheet_ref.shape, jnp.float32)
    for s in range(slots):
        mine = sorted_ref[pl.ds(s, cands // slots, stride=slots), :]
        total = jnp.sum(mine, axis=1, keepdims=True) * weight_scale
        sheet = jnp.where(lane == rnd * slots + s, total, sheet)
    cost = jnp.sum(out_run_ref[...], axis=1, keepdims=True) * cost_scale
    out_sheet_ref[...] = jnp.where(lane == COST_LANE + rnd, cost, sheet)


def run_round(pieces, frames, sq, running, sheet, owner, counts, rnd, slots, factor, devices):
    fr_dev, width = frames.shape
    cands = sum(p.shape[0] for p in pieces)
    vmem = pl.BlockSpec(memory_space=pltpu.VMEM)
    smem = pl.BlockSpec(memory_space=pltpu.SMEM)
    kernel = functools.partial(
        round_kernel, slots, factor, rnd, slots / fr_dev, 1.0 / (fr_dev * devices * width), len(pieces)
    )
    return pl.pallas_call(
        kernel,
        out_shape=(
            jax.ShapeDtypeStruct((1, fr_dev), jnp.float32),
            jax.ShapeDtypeStruct(sheet.shape, jnp.float32),
        ),
        in_specs=[smem, smem] + [vmem] * (len(pieces) + 4),
        out_specs=(vmem, vmem),
        scratch_shapes=[
            pltpu.VMEM((width // 128, cands + slots, 128), jnp.float32),
            pltpu.VMEM((cands, width), jnp.bfloat16),
            pltpu.VMEM((cands, LANES), jnp.float32),
            pltpu.VMEM((cands, LANES), jnp.float32),
            pltpu.VMEM((cands, 128), jnp.float32),
            pltpu.VMEM((cands + slots, 128), jnp.float32),
            pltpu.VMEM((cands, 128), jnp.float32),
        ],
        compiler_params=pltpu.CompilerParams(vmem_limit_bytes=28 * 1024 * 1024),
        cost_estimate=pl.CostEstimate(
            flops=2 * cands * fr_dev * width,
            bytes_accessed=8 * 1024 * 1024,
            transcendentals=cands * fr_dev,
        ),
    )(owner, counts, *pieces, frames, sq, running, sheet)


def pick_kernel(index_ref, frames_ref, out_ref, near_ref, row_ref, sems):
    rounds, _, slots = index_ref.shape
    wanted = [index_ref[r, 0, s] for r in range(rounds) for s in range(slots)]
    copies = []
    for i, at in enumerate(wanted):
        rows = pl.ds(pl.multiple_of((at // 16) * 16, 16), 16)
        copies.append(pltpu.make_async_copy(frames_ref.at[rows], near_ref.at[i], sems.at[i]))
        copies[-1].start()
    row = lax.broadcasted_iota(jnp.int32, (16, frames_ref.shape[1]), 0)
    for i, at in enumerate(wanted):
        copies[i].wait()
        near = near_ref[i].astype(jnp.float32)
        row_ref[i:i + 1, :] = jnp.sum(jnp.where(row == at % 16, near, 0.0), axis=0, keepdims=True)
    rows = row_ref[...].astype(jnp.bfloat16)
    for member in range(out_ref.shape[0]):
        out_ref[member] = rows


def pick_rows(frames, cand_index, members):
    count, width = cand_index.shape[0] * cand_index.shape[2], frames.shape[1]
    return pl.pallas_call(
        pick_kernel,
        out_shape=jax.ShapeDtypeStruct((members, count, width), frames.dtype),
        in_specs=[pl.BlockSpec(memory_space=pltpu.SMEM), pl.BlockSpec(memory_space=pl.ANY)],
        out_specs=pl.BlockSpec(memory_space=pltpu.VMEM),
        scratch_shapes=[
            pltpu.VMEM((count, 16, width), frames.dtype),
            pltpu.VMEM((count, width), jnp.float32),
            pltpu.SemaphoreType.DMA((count,)),
        ],
        compiler_params=pltpu.CompilerParams(vmem_limit_bytes=60 * 1024 * 1024),
        cost_estimate=pl.CostEstimate(flops=0, bytes_accessed=1024 * 1024, transcendentals=0),
    )(cand_index, frames)


def body(frames, min_dist, cand_index, cand_count):
    fr_dev, width = frames.shape
    rounds, _, slots = cand_index.shape
    devices = lax.axis_size("dp")
    me = lax.axis_index("dp")
    factor = 16.0 / width

    groups = plane_groups()
    members = len(groups[0])
    rows = pick_rows(frames, cand_index, members).reshape(members * rounds * slots, width)
    block = lax.all_to_all(rows, "dp", 0, 0, axis_index_groups=groups, tiled=True)
    block, frames = lax.optimization_barrier((block, frames))
    own = [block, lax.ppermute(block, "dp", swap_perm())]
    own = [b.reshape(members, rounds, slots, width) for b in own]
    parts = [[b[:, r].reshape(members * slots, width) for b in own] for r in range(rounds)]

    sq = jnp.sum(jnp.square(frames.astype(jnp.float32)), axis=1).reshape(1, fr_dev)
    scaled = frames * jnp.bfloat16(-2.0)
    owner = lax.dynamic_slice_in_dim(jnp.asarray(owner_table()), me, 1, 0)

    running = min_dist.reshape(1, fr_dev)
    sheet = jnp.zeros((devices, 128), jnp.float32)
    gathered = []
    for r in range(rounds):
        part, swapped = parts[r]
        if r > 0:
            part, _ = lax.optimization_barrier((part, gathered[-1][1]))
        mine = last_stage(part)
        if r == 0:
            mine[1], sq, scaled, owner = lax.optimization_barrier((mine[1], sq, scaled, owner))
        else:
            arrived, sheet = lax.optimization_barrier((mine[1:], sheet))
            mine = mine[:1] + list(arrived)
        theirs = [swapped] + [lax.ppermute(p, "dp", swap_perm()) for p in mine[1:]]
        gathered.append(mine)
        running, sheet = run_round(
            mine + theirs, scaled, sq, running, sheet, owner, cand_count, r, slots, factor, devices
        )
    sums = jnp.sum(lax.all_to_all(sheet, "dp", 0, 0, tiled=True), axis=0)
    mine = sums[: rounds * slots].reshape(rounds, slots)
    return (running.reshape(fr_dev), mine, sums[COST_LANE:COST_LANE + rounds])


def solution(mesh):
    return jax.shard_map(
        body,
        mesh=mesh,
        in_specs=(P("dp", None), P("dp"), P(None, "dp", None), P()),
        out_specs=(P("dp"), P(None, "dp"), P()),
        check_vma=False,
    )
```

```python
import functools
import math

import jax
import jax.numpy as jnp
import numpy as np
from jax import lax
from jax.experimental import pallas as pl
from jax.experimental.pallas import tpu as pltpu
from jax.sharding import PartitionSpec as P

DIMS = (4, 4, 4)
CORES = 2
LAST = (0, 1)
OFFSETS = (0, 2, -1, 1)


def device_id(pos, core):
    return ((pos[0] * DIMS[1] + pos[1]) * DIMS[2] + pos[2]) * CORES + core


def all_positions():
    for z in range(DIMS[0]):
        for x in range(DIMS[1]):
            for y in range(DIMS[2]):
                yield (z, x, y)


def moved(pos, axis, by):
    out = list(pos)
    out[axis] = (out[axis] + by) % DIMS[axis]
    return tuple(out)


def plane(pos, axis):
    return [p for p in all_positions() if p[axis] == pos[axis]]


def plane_groups():
    groups = []
    for core in range(CORES):
        for at in range(DIMS[LAST[core]]):
            pos = moved((0, 0, 0), LAST[core], at)
            groups.append([device_id(p, core) for p in plane(pos, LAST[core])])
    return groups


def last_perm(offset):
    pairs = []
    for pos in all_positions():
        for core in range(CORES):
            source = moved(pos, LAST[core], offset)
            pairs.append((device_id(source, core), device_id(pos, core)))
    return pairs


def swap_perm():
    return [
        (device_id(pos, core), device_id(pos, 1 - core))
        for pos in all_positions()
        for core in range(CORES)
    ]


def owner_table():
    table = np.zeros((DIMS[0] * DIMS[1] * DIMS[2] * CORES,) * 2, np.int32)
    for pos in all_positions():
        for core in range(CORES):
            row = []
            for parity in (core, 1 - core):
                for offset in OFFSETS:
                    there = moved(pos, LAST[parity], offset)
                    row += [device_id(p, parity) for p in plane(there, LAST[parity])]
            table[device_id(pos, core)] = row
    return table


def last_stage(block):
    return [block] + [lax.ppermute(block, "dp", last_perm(off)) for off in OFFSETS[1:]]


LANES = 256
COST_LANE = 120
SIZES = (1152, 1280)


def fold_rows(x, op):
    parts = [x[k * 8:(k + 1) * 8, :] for k in range(x.shape[0] // 8)]
    while len(parts) > 1:
        paired = [op(a, b) for a, b in zip(parts[::2], parts[1::2])]
        parts = paired + parts[len(parts) - len(parts) % 2:]
    return parts[0]


def round_kernel(slots, factor, rnd, weight_scale, cost_scale, n_pieces, owner_ref, count_ref, *refs):
    pieces, refs = refs[:n_pieces], refs[n_pieces:]
    frame_ref, sq_ref, run_ref, sheet_ref, out_run_ref, out_sheet_ref = refs[:6]
    wide_ref, cand_ref, even_ref, odd_ref, norm_ref, acc_ref, sorted_ref = refs[6:]
    cands, width = cand_ref.shape
    rows_each = cands // n_pieces
    blocks = frame_ref.shape[0] // LANES
    groups = rows_each // slots

    live = jnp.int32(0)
    for j, piece in enumerate(pieces):
        def close_up(g, at, j=j, piece=piece):
            rows = piece[pl.ds(pl.multiple_of(g * slots, slots), slots), :].astype(jnp.float32)
            for k in range(width // 128):
                wide_ref[k, pl.ds(at, slots), :] = rows[:, k * 128:(k + 1) * 128]
            return at + count_ref[rnd, owner_ref[0, j * groups + g]]

        live = lax.fori_loop(0, groups, close_up, live, unroll=16)
    scale = factor * math.log2(math.e)

    def lanes(t):
        return pl.ds(pl.multiple_of(t * LANES, LANES), LANES)

    def all_blocks(size):
        chunk = size // 2
        part_rows = 128

        def narrow(i, carry):
            at = pl.multiple_of(i * part_rows, part_rows)
            kept = lax.broadcasted_iota(jnp.int32, (part_rows, 128), 0) + at < live
            squares = jnp.zeros((part_rows, 128), jnp.float32)
            for k in range(width // 128):
                x = jnp.where(kept, wide_ref[k, pl.ds(at, part_rows), :], 0.0)
                cand_ref[pl.ds(at, part_rows), k * 128:(k + 1) * 128] = x.astype(jnp.bfloat16)
                squares = squares + x * x
            norm = jnp.broadcast_to(jnp.sum(squares, axis=1, keepdims=True), (part_rows, 128))
            norm_ref[pl.ds(at, part_rows), :] = jnp.where(kept, norm, jnp.inf)
            acc_ref[pl.ds(at, part_rows), :] = jnp.zeros((part_rows, 128), jnp.float32)
            return carry

        parts = size // part_rows
        lax.fori_loop(0, parts, narrow, 0, unroll=parts if parts < 10 else 2)

        def step(t, near, into, of):
            if into is not None:
                part = frame_ref[lanes(t + 1), :]
                sq = sq_ref[:, lanes(t + 1)]
                lowest = jnp.full((8, LANES), jnp.inf, jnp.float32)
            total = jnp.zeros((8, LANES), jnp.float32)
            for first in range(0, size, chunk):
                if into is not None:
                    rows = slice(first, first + chunk)
                    inner = lax.dot_general(
                        cand_ref[rows, :], part, (((1,), (1,)), ((), ())),
                        preferred_element_type=jnp.float32,
                    )
                    norm = norm_ref[rows, :]
                    norm = jnp.concatenate([norm, norm], axis=1)
                    dist = jnp.maximum((norm + sq) + inner, 0.0)
                    into[rows, :] = dist
                    lowest = jnp.minimum(lowest, fold_rows(dist, jnp.minimum))
                if of is not None:
                    for r in range(first, first + chunk, chunk // 4):
                        e = jnp.exp2((near - of[r:r + chunk // 4, :]) * scale)
                        of[r:r + chunk // 4, :] = e
                        total = total + fold_rows(e, jnp.add)
            if of is not None:
                recip = 1.0 / jnp.sum(total, axis=0, keepdims=True)
                for r in range(0, size, chunk // 4):
                    share = of[r:r + chunk // 4, :] * recip
                    acc_ref[r:r + chunk // 4, :] += share[:, :128] + share[:, 128:]
            if into is None:
                return None
            near = jnp.min(lowest, axis=0, keepdims=True)
            out_run_ref[:, lanes(t + 1)] = jnp.minimum(run_ref[:, lanes(t + 1)], near)
            return near

        def pair(i, near):
            near = step(2 * i, near, odd_ref, even_ref)
            return step(2 * i + 1, near, even_ref, odd_ref)

        near = step(-1, None, even_ref, None)
        near = lax.fori_loop(0, blocks // 2 - 1, pair, near)
        near = step(blocks - 2, near, odd_ref, even_ref)
        step(blocks - 1, near, None, odd_ref)

    above = jnp.int32(0)
    for size in [s for s in SIZES if s < cands] + [cands]:
        pl.when(jnp.logical_and(live > above, live <= size))(functools.partial(all_blocks, size))
        above = size

    slot = lax.broadcasted_iota(jnp.int32, (slots, 128), 0)

    def place(g, at):
        to = pl.multiple_of(owner_ref[0, g] * slots, slots)
        limit = count_ref[rnd, owner_ref[0, g]]
        mine = acc_ref[pl.ds(at, slots), :]
        sorted_ref[pl.ds(to, slots), :] = jnp.where(slot < limit, mine, 0.0)
        return at + limit

    lax.fori_loop(0, cands // slots, place, jnp.int32(0), unroll=16)
    lane = lax.broadcasted_iota(jnp.int32, sheet_ref.shape, 1)
    sheet = sheet_ref[...] if rnd > 0 else jnp.zeros(sheet_ref.shape, jnp.float32)
    for s in range(slots):
        mine = sorted_ref[pl.ds(s, cands // slots, stride=slots), :]
        total = jnp.sum(mine, axis=1, keepdims=True) * weight_scale
        sheet = jnp.where(lane == rnd * slots + s, total, sheet)
    cost = jnp.sum(out_run_ref[...], axis=1, keepdims=True) * cost_scale
    out_sheet_ref[...] = jnp.where(lane == COST_LANE + rnd, cost, sheet)


def run_round(pieces, frames, sq, running, sheet, owner, counts, rnd, slots, factor, devices):
    fr_dev, width = frames.shape
    cands = sum(p.shape[0] for p in pieces)
    vmem = pl.BlockSpec(memory_space=pltpu.VMEM)
    smem = pl.BlockSpec(memory_space=pltpu.SMEM)
    kernel = functools.partial(
        round_kernel, slots, factor, rnd, slots / fr_dev, 1.0 / (fr_dev * devices * width), len(pieces)
    )
    return pl.pallas_call(
        kernel,
        out_shape=(
            jax.ShapeDtypeStruct((1, fr_dev), jnp.float32),
            jax.ShapeDtypeStruct(sheet.shape, jnp.float32),
        ),
        in_specs=[smem, smem] + [vmem] * (len(pieces) + 4),
        out_specs=(vmem, vmem),
        scratch_shapes=[
            pltpu.VMEM((width // 128, cands + slots, 128), jnp.float32),
            pltpu.VMEM((cands, width), jnp.bfloat16),
            pltpu.VMEM((cands, LANES), jnp.float32),
            pltpu.VMEM((cands, LANES), jnp.float32),
            pltpu.VMEM((cands, 128), jnp.float32),
            pltpu.VMEM((cands + slots, 128), jnp.float32),
            pltpu.VMEM((cands, 128), jnp.float32),
        ],
        compiler_params=pltpu.CompilerParams(vmem_limit_bytes=28 * 1024 * 1024),
        cost_estimate=pl.CostEstimate(
            flops=2 * cands * fr_dev * width,
            bytes_accessed=8 * 1024 * 1024,
            transcendentals=cands * fr_dev,
        ),
    )(owner, counts, *pieces, frames, sq, running, sheet)


def pick_kernel(index_ref, frames_ref, out_ref, near_ref, row_ref, sems):
    rounds, _, slots = index_ref.shape
    wanted = [index_ref[r, 0, s] for r in range(rounds) for s in range(slots)]
    copies = []
    for i, at in enumerate(wanted):
        rows = pl.ds(pl.multiple_of((at // 16) * 16, 16), 16)
        copies.append(pltpu.make_async_copy(frames_ref.at[rows], near_ref.at[i], sems.at[i]))
        copies[-1].start()
    row = lax.broadcasted_iota(jnp.int32, (16, frames_ref.shape[1]), 0)
    for i, at in enumerate(wanted):
        copies[i].wait()
        near = near_ref[i].astype(jnp.float32)
        row_ref[i:i + 1, :] = jnp.sum(jnp.where(row == at % 16, near, 0.0), axis=0, keepdims=True)
    rows = row_ref[...].astype(jnp.bfloat16)
    for member in range(out_ref.shape[0]):
        out_ref[member] = rows


def pick_rows(frames, cand_index, members):
    count, width = cand_index.shape[0] * cand_index.shape[2], frames.shape[1]
    return pl.pallas_call(
        pick_kernel,
        out_shape=jax.ShapeDtypeStruct((members, count, width), frames.dtype),
        in_specs=[pl.BlockSpec(memory_space=pltpu.SMEM), pl.BlockSpec(memory_space=pl.ANY)],
        out_specs=pl.BlockSpec(memory_space=pltpu.VMEM),
        scratch_shapes=[
            pltpu.VMEM((count, 16, width), frames.dtype),
            pltpu.VMEM((count, width), jnp.float32),
            pltpu.SemaphoreType.DMA((count,)),
        ],
        compiler_params=pltpu.CompilerParams(vmem_limit_bytes=60 * 1024 * 1024),
        cost_estimate=pl.CostEstimate(flops=0, bytes_accessed=1024 * 1024, transcendentals=0),
    )(cand_index, frames)


def body(frames, min_dist, cand_index, cand_count):
    fr_dev, width = frames.shape
    rounds, _, slots = cand_index.shape
    devices = lax.axis_size("dp")
    me = lax.axis_index("dp")
    factor = 16.0 / width

    groups = plane_groups()
    members = len(groups[0])
    rows = pick_rows(frames, cand_index, members).reshape(members * rounds * slots, width)
    block = lax.all_to_all(rows, "dp", 0, 0, axis_index_groups=groups, tiled=True)
    block, frames = lax.optimization_barrier((block, frames))
    own = [block, lax.ppermute(block, "dp", swap_perm())]
    own = [b.reshape(members, rounds, slots, width) for b in own]
    parts = [[b[:, r].reshape(members * slots, width) for b in own] for r in range(rounds)]

    sq = jnp.sum(jnp.square(frames.astype(jnp.float32)), axis=1).reshape(1, fr_dev)
    scaled = frames * jnp.bfloat16(-2.0)
    owner = lax.dynamic_slice_in_dim(jnp.asarray(owner_table()), me, 1, 0)

    running = min_dist.reshape(1, fr_dev)
    sheet = jnp.zeros((devices, 128), jnp.float32)
    gathered = []
    for r in range(rounds):
        part, swapped = parts[r]
        if r > 0:
            part, _ = lax.optimization_barrier((part, gathered[-1][1]))
        mine = last_stage(part)
        if r == 0:
            mine[1], sq, scaled, owner = lax.optimization_barrier((mine[1], sq, scaled, owner))
        else:
            arrived, sheet = lax.optimization_barrier((mine[1:], sheet))
            mine = mine[:1] + list(arrived)
        theirs = [swapped] + [lax.ppermute(p, "dp", swap_perm()) for p in mine[1:]]
        gathered.append(mine)
        running, sheet = run_round(
            mine + theirs, scaled, sq, running, sheet, owner, cand_count, r, slots, factor, devices
        )
    sums = jnp.sum(lax.all_to_all(sheet, "dp", 0, 0, tiled=True), axis=0)
    mine = sums[: rounds * slots].reshape(rounds, slots)
    return (running.reshape(fr_dev), mine, sums[COST_LANE:COST_LANE + rounds])


def solution(mesh):
    return jax.shard_map(
        body,
        mesh=mesh,
        in_specs=(P("dp", None), P("dp"), P(None, "dp", None), P()),
        out_specs=(P("dp"), P(None, "dp"), P()),
        check_vma=False,
    )
```
